32 devices in a mesh: ctx: 16 (over z, y, core), tp: 2 (over x).
Axes of the slice: x: 2, y: 2, z: 4, core: 2. Of those that a mesh axis runs over, the one named last changes fastest.
Arguments:
- tokens: bfloat16 [16384, 1024], P('ctx', 'tp'), may hold values from -6 to 6
- view_counts: int32 [4], replicated, may hold values from 1 to 9, 16 in all
- ln_gain: float32 [1024], replicated, may hold values from 0.25 to 1.75
- w_qkv: bfloat16 [3, 1024, 1024], P(None, None, 'tp'), may hold values from -0.1875 to 0.1875
- head_temp: float32 [16], P('tp'), may hold values from 0.5 to 64
- o_gain: float32 [1024], P('tp'), may hold values from 0.1 to 1.9
- w_o: bfloat16 [1024, 1024], P('tp'), may hold values from -0.25 to 0.25
Outputs:
- mixed: bfloat16 [16384, 1024], P('ctx', 'tp')
The draws below stay inside these ranges and needn't reach their ends.
Inputs may be any that keep to these rules, and one draw needn't show every extreme that they name: `view_counts`: the view counts sum to 16; the largest is exactly 9.
All inputs are finite; a program needn't handle non-finite values.
Results may differ from the reference program's by a relative error of at most 0.01.
The reference program's roundings to bfloat16 on the way (of `normed`, `weight` and `heads_out`) count: a program that leaves them out, or rounds other values in their place, can miss the bound.
Values may be sent and summed in bfloat16 or wider, within the bound.
A program may use at most 1 GiB of HBM per device.

```python
import math
import jax
import jax.numpy as jnp
import numpy as np
from jax import lax

D = 1024
HEADS = 16
HEAD_DIM = 64
VIEW_TOK = 1024
SCENES = 4
VIEWS = 16
MOST_VIEWS = 9
TOKENS = 16384


def draw_head_temp(key, part):
    spread = jax.random.uniform(jax.random.fold_in(key, 11), (HEADS,), jnp.float32, 0.0, 1.0)
    temps = jnp.exp(jnp.log(0.5) + spread * (jnp.log(4.0) - jnp.log(0.5)))
    return temps.astype(jnp.float32)


def with_spikes(array, own_key, source, target, shards_of, factor):
    owner, partner = [(jnp.arange(array.shape[axis_at]) // (array.shape[axis_at] // shards_of)).reshape([-1 if axis == axis_at else 1 for axis in range(array.ndim)]) for axis_at in (source, target)]
    chosen = jax.random.permutation(own_key, shards_of)[partner]
    strong = (owner == chosen) | (owner == (partner + shards_of // 2) % shards_of)
    return jnp.where(strong, factor * array, array)


def shard_levels(rng, dims, pieces, least, high):
    factor_of = 1.0
    for axis_at, parts in pieces:
        draws = jax.random.uniform(jax.random.fold_in(jax.random.fold_in(rng, 6), axis_at), (parts,), jnp.float32, least / len(pieces), high / len(pieces))
        factor_of = factor_of * jnp.repeat(jnp.exp(draws), dims[axis_at] // parts).reshape((-1,) + (1,) * (len(dims) - 1 - axis_at))
    return factor_of


def profile(count, total, most, slope):
    weights = [(1 << 20) // math.isqrt(rank ** slope) + 1 for rank in range(2, count + 1)]
    rest, given = total - most - (count - 1), [1] * (count - 1)
    while rest > 0:
        free = [i for i in range(count - 1) if given[i] < most]
        pool, remaining = sum([weights[i] for i in free]), rest
        for i in free:
            more = min(most - given[i], max(1, remaining * weights[i] // pool), rest)
            given[i] = given[i] + more
            rest = rest - more
    return np.array([most] + given)


def ragged_sizes(own_key, amount, total, limit, slope):
    if amount == 2:
        one = jax.random.randint(own_key, (), max(1, total - limit), min(limit, total - 1) + 1)
        return jnp.stack([one, total - one])
    lengths = jnp.asarray(profile(amount, total, limit, slope), jnp.int32)
    pairs = (amount - 1) // 2
    giver, sink = lengths[1:1 + 2 * pairs:2], lengths[2:2 + 2 * pairs:2]
    room = jnp.minimum(giver - 1, limit - sink)
    passed = jax.random.randint(jax.random.fold_in(own_key, 1), (pairs,), 0, 1 << 20) % (room + 1)
    lengths = lengths.at[1:1 + 2 * pairs:2].set(giver - passed).at[2:2 + 2 * pairs:2].set(sink + passed)
    return lengths[jax.random.permutation(jax.random.fold_in(own_key, 2), amount)]


def bell_draw(stream_key, shape, width, limit, shards=(), kind=jnp.bfloat16):
    values = jax.random.normal(stream_key, shape, jnp.float32) * width
    if len(shards) > 0:
        values = shard_levels(stream_key, shape, shards, -0.22, 0.18) * values
    return jnp.clip(values, min=-limit, max=limit).astype(kind)


def gaussian_with(own_key, shape, scale, most, shards, heavy, kind=jnp.bfloat16):
    array = scale * jax.random.normal(own_key, shape, jnp.float32)
    if shards:
        array = array * shard_levels(own_key, shape, shards, -0.22, 0.18)
    return jnp.clip(with_spikes(array, jax.random.fold_in(own_key, 3), *heavy), -most, most).astype(kind)


def setup_inputs(seed: int = 0) -> dict:
    key_list = jax.random.split(jax.random.key(seed), 8)
    tokens = bell_draw(key_list[0], (TOKENS, D), 1.0, 6.0, ((0, 16), (1, 2)))
    view_counts = ragged_sizes(key_list[1], SCENES, VIEWS, MOST_VIEWS, 2).astype(jnp.int32)
    ln_gain = jnp.clip(1.0 + 0.15 * jax.random.normal(key_list[2], (D,), jnp.float32), 0.25, 1.75)
    w_qkv = bell_draw(key_list[3], (3, D, D), D ** -0.5, 0.1875, ((2, 2),))
    head_temp = draw_head_temp(jax.random.fold_in(key_list[7], 71), 0)
    o_gain = jnp.clip(1.0 + 0.18 * jax.random.normal(key_list[5], (D,), jnp.float32), 0.1, 1.9)
    w_o = gaussian_with(key_list[6], (D, D), D ** -0.5, 0.25, ((0, 2),), (0, 1, 2, 2.0))
    return dict(tokens=tokens, view_counts=view_counts, ln_gain=ln_gain, w_qkv=w_qkv, head_temp=head_temp, o_gain=o_gain, w_o=w_o)


def scene_of_views(view_counts):
    ends = jnp.cumsum(view_counts)
    views = jnp.arange(VIEWS, dtype=jnp.int32)
    return lax.optimization_barrier(jnp.sum((ends[None, :] <= views[:, None]).astype(jnp.int32), axis=1))

def reference(tokens, view_counts, ln_gain, w_qkv, head_temp, o_gain, w_o):
    xfull = tokens.astype(jnp.float32)
    center = xfull - lax.optimization_barrier(jnp.mean(xfull, axis=-1, keepdims=True))
    spread = lax.optimization_barrier(jnp.mean(center * center, axis=-1, keepdims=True))
    normed = (center * lax.rsqrt(spread + 1e-05) * ln_gain).astype(jnp.bfloat16)
    query = jnp.dot(normed, w_qkv[0], preferred_element_type=jnp.float32).astype(jnp.bfloat16)
    keys = jnp.dot(normed, w_qkv[1], preferred_element_type=jnp.float32).astype(jnp.bfloat16)
    values = jnp.dot(normed, w_qkv[2], preferred_element_type=jnp.float32).astype(jnp.bfloat16)
    query = query.reshape(VIEWS, VIEW_TOK, HEADS, HEAD_DIM)
    keys = keys.reshape(VIEWS, VIEW_TOK, HEADS, HEAD_DIM).astype(jnp.float32)
    values = values.reshape(VIEWS, VIEW_TOK, HEADS, HEAD_DIM).astype(jnp.float32)
    scene = scene_of_views(view_counts)
    scale = head_temp / math.sqrt(HEAD_DIM)
    gains = o_gain.reshape(HEADS, HEAD_DIM)

    def one_view(index):
        qview = query[index].astype(jnp.float32)
        score = jnp.einsum('qhd,vkhd->hqvk', qview, keys) * scale[:, None, None, None]
        allowed = (scene == scene[index])[None, None, :, None]
        score = jnp.where(allowed, score, -1e+30)
        top = lax.optimization_barrier(jnp.max(score, axis=(2, 3), keepdims=True))
        weight = jnp.where(allowed, jnp.exp(score - top), 0.0)
        total = lax.optimization_barrier(jnp.sum(weight, axis=(2, 3)))
        rounded = weight.astype(jnp.bfloat16).astype(jnp.float32)
        attended = jnp.einsum('hqvk,vkhd->qhd', rounded, values) / jnp.transpose(total)[:, :, None]
        level = lax.optimization_barrier(jnp.mean(attended * attended, axis=-1, keepdims=True))
        heads_out = attended * lax.rsqrt(level + 1e-05) * gains[None, :, :]
        return heads_out.reshape(VIEW_TOK, D).astype(jnp.bfloat16)
    heads_out = lax.map(one_view, jnp.arange(VIEWS, dtype=jnp.int32)).reshape(TOKENS, D)
    mixed = jnp.dot(heads_out, w_o, preferred_element_type=jnp.float32) + xfull
    return mixed.astype(jnp.bfloat16)
```

```python
import functools
import math

import jax
import jax.numpy as jnp
from jax import lax
from jax.experimental import pallas as pl
from jax.experimental.pallas import tpu as pltpu
from jax.sharding import PartitionSpec as P

BF16 = jnp.bfloat16
F32 = jnp.float32
LOG2E = 1.4426950408889634
LANES = 128
ROW_TILE = 256


def attention_kernel(hs, span, c_ref, q_ref, k_ref, v_ref, g_ref, o_ref, q_s, top_s, acc_s):
    j = pl.program_id(0)
    rows, width = q_ref.shape
    per = width // hs
    tile = min(ROW_TILE, rows)
    lane = lax.broadcasted_iota(jnp.int32, (rows, width), 1) // hs

    @pl.when(j == 0)
    def _():
        for h in range(per):
            q_s[h] = jnp.where(lane == h, q_ref[...], jnp.zeros((), BF16))
        top_s[...] = jnp.full_like(top_s, -1e30)
        acc_s[...] = jnp.zeros_like(acc_s)

    @pl.when(j < span[1])
    def _():
        keys = k_ref[...]
        values = [jnp.where(lane == h, v_ref[...], jnp.ones((), BF16)) for h in range(per)]
        steps = [(h, i) for i in range(rows // tile) for h in range(per)]

        def score(h, i):
            return lax.dot_general(
                q_s[h, pl.ds(i * tile, tile), :],
                keys,
                (((1,), (1,)), ((), ())),
                preferred_element_type=F32,
            )

        after = score(*steps[0])
        for n, (h, i) in enumerate(steps):
            s = after
            if n + 1 < len(steps):
                after = score(*steps[n + 1])
            at = pl.ds(i * tile, tile)
            old = top_s[h, at, :]
            new = jnp.maximum(old, jnp.max(s, axis=1, keepdims=True))
            top_s[h, at, :] = new
            shrink = jnp.exp2((old - new) * c_ref[h])
            p = jnp.exp2((s - new[:, :1]) * c_ref[h]).astype(BF16)
            term = jnp.dot(p, values[h], preferred_element_type=F32)
            acc_s[h, at, :] = acc_s[h, at, :] * shrink + term

    @pl.when(j == pl.num_programs(0) - 1)
    def _():
        out = jnp.zeros((rows, width), F32)
        for h in range(per):
            acc = acc_s[h]
            total = acc[:, ((h + 1) % per) * hs : ((h + 1) % per) * hs + 1]
            attended = jnp.where(lane == h, acc / total, 0.0)
            level = jnp.sum(attended * attended, axis=1, keepdims=True) / hs
            out = out + attended * lax.rsqrt(level + 1e-05)
        o_ref[...] = (out * g_ref[...]).astype(BF16)


def attention(span, c, query, kv, gain, hs, busy):
    rows, width = query.shape
    views = kv.shape[0] // rows
    per = width // hs

    def view(j, s):
        return s[0] + jnp.minimum(j, s[1] - 1)

    return pl.pallas_call(
        functools.partial(attention_kernel, hs),
        out_shape=jax.ShapeDtypeStruct((rows, width), BF16),
        grid_spec=pltpu.PrefetchScalarGridSpec(
            num_scalar_prefetch=1,
            grid=(views,),
            in_specs=[
                pl.BlockSpec(memory_space=pltpu.SMEM),
                pl.BlockSpec((rows, width), lambda j, s: (0, 0)),
                pl.BlockSpec((rows, width), lambda j, s: (view(j, s), 0)),
                pl.BlockSpec((rows, width), lambda j, s: (view(j, s), 1)),
                pl.BlockSpec((1, width), lambda j, s: (0, 0)),
            ],
            out_specs=pl.BlockSpec((rows, width), lambda j, s: (0, 0)),
            scratch_shapes=[
                pltpu.VMEM((per, rows, width), BF16),
                pltpu.VMEM((per, rows, LANES), F32),
                pltpu.VMEM((per, rows, width), F32),
            ],
        ),
        compiler_params=pltpu.CompilerParams(vmem_limit_bytes=48 << 20),
        cost_estimate=pl.CostEstimate(
            flops=8 * rows * rows * busy * width * per,
            bytes_accessed=4 * rows * busy * width,
            transcendentals=rows * rows * busy * per,
        ),
    )(span, c, query, kv, kv, gain)


def body(tp, tokens, view_counts, ln_gain, w_qkv, head_temp, o_gain, w_o):
    rows, part = tokens.shape
    me = lax.axis_index("tp")
    swap = [(0, 1), (1, 0)]
    if tp == 2:
        other = lax.ppermute(tokens, "tp", swap)
        whole = jnp.where(
            me == 0,
            jnp.concatenate([tokens, other], axis=1),
            jnp.concatenate([other, tokens], axis=1),
        )
    else:
        whole = lax.all_gather(tokens, "tp", axis=1, tiled=True)
    xfull = whole.astype(F32)
    center = xfull - jnp.mean(xfull, axis=-1, keepdims=True)
    spread = jnp.mean(center * center, axis=-1, keepdims=True)
    normed = (center * lax.rsqrt(spread + 1e-05) * ln_gain).astype(BF16)

    heads_here = head_temp.shape[0]
    width = w_qkv.shape[2]
    hs = width // heads_here
    per = LANES // hs
    chunks = width // LANES
    ends = jnp.cumsum(view_counts)
    own_view = lax.axis_index("ctx")
    own_scene = jnp.sum((ends <= own_view).astype(jnp.int32))
    count = view_counts[own_scene]
    span = jnp.stack([ends[own_scene] - count, count]).astype(jnp.int32)
    c = head_temp * (LOG2E / math.sqrt(hs))

    def cut(array, i):
        return lax.slice_in_dim(array, i * LANES, (i + 1) * LANES, axis=-1)

    queries, gathered = [], []
    for i in range(chunks):
        w_kv = jnp.concatenate([cut(w_qkv[1], i), cut(w_qkv[2], i)], axis=1)
        kv = jnp.dot(normed, w_kv, preferred_element_type=F32).astype(BF16)
        if gathered:
            kv, gathered[-1] = lax.optimization_barrier((kv, gathered[-1]))
        gathered.append(lax.all_gather(kv, "ctx", axis=0, tiled=True))
    query = jnp.dot(normed, w_qkv[0], preferred_element_type=F32).astype(BF16)
    queries = [cut(query, i) for i in range(chunks)]
    views = lax.axis_size("ctx")

    if tp == 2:
        out_here = lax.dynamic_slice_in_dim(w_o, me * part, part, axis=1)
        out_there = lax.dynamic_slice_in_dim(w_o, (1 - me) * part, part, axis=1)
        out_there, _ = lax.optimization_barrier((out_there, whole))
        out_there = lax.ppermute(out_there, "tp", swap)
    total = tokens.astype(F32)
    outs = []
    for i in range(chunks):
        heads = attention(
            span,
            c[i * per : (i + 1) * per],
            queries[i],
            gathered[i],
            o_gain[i * LANES : (i + 1) * LANES].reshape(1, LANES),
            hs,
            views // 2 + 1,
        )
        if tp == 2:
            at = slice(i * LANES, (i + 1) * LANES)
            received = lax.ppermute(heads, "tp", swap)
            total = total + jnp.dot(heads, out_here[at], preferred_element_type=F32)
            total = total + jnp.dot(received, out_there[at], preferred_element_type=F32)
        else:
            outs.append(heads)
    if tp != 2:
        heads_out = jnp.concatenate(outs, axis=1)
        terms = jnp.dot(heads_out, w_o, preferred_element_type=F32)
        total = total + lax.psum_scatter(
            terms.astype(BF16), "tp", scatter_dimension=1, tiled=True
        ).astype(F32)
    return total.astype(BF16)


def solution(mesh):
    in_specs = (P("ctx", "tp"), P(), P(), P(None, None, "tp"), P("tp"), P("tp"), P("tp", None))
    out_specs = P("ctx", "tp")
    return jax.shard_map(
        functools.partial(body, mesh.shape["tp"]),
        mesh=mesh,
        in_specs=in_specs,
        out_specs=out_specs,
        check_vma=False,
    )
```

```python
import functools
import math

import jax
import jax.numpy as jnp
from jax import lax
from jax.experimental import pallas as pl
from jax.experimental.pallas import tpu as pltpu
from jax.sharding import PartitionSpec as P

BF16 = jnp.bfloat16
F32 = jnp.float32
LOG2E = 1.4426950408889634


def attention_kernel(hs, span, c_ref, g_ref, got_ref, *rest):
    *others, o_ref, s_s, top_s, acc_s = rest
    i = pl.program_id(0)
    tile, lanes = o_ref.shape[1:]
    part = got_ref.shape[1] - tile
    first = lax.broadcasted_iota(jnp.int32, (tile, lanes), 1) < hs
    packed = got_ref[i, part:, :].astype(F32)
    queries = [
        jnp.where(first, x, 0.0).astype(BF16) for x in (packed, pltpu.roll(packed, hs, 1))
    ]
    low, count = span[0, i], span[1, i]

    def pairs(j):
        return jnp.concatenate([got_ref[j, :part, :]] + [ref[j] for ref in others], axis=0)

    def score(query, kv):
        return lax.dot_general(
            query, kv, (((1,), (1,)), ((), ())), preferred_element_type=F32
        )

    top_s[...] = jnp.full_like(top_s, -1e30)
    acc_s[...] = jnp.zeros_like(acc_s)
    s_s[...] = score(queries[0], pairs(low))

    def step(n, carry):
        kv = pairs(low + n)
        key_lanes = lax.broadcasted_iota(jnp.int32, kv.shape, 1) < hs
        values = jnp.where(key_lanes, jnp.ones((), BF16), kv)

        def update(t, s):
            old = top_s[t]
            new = jnp.maximum(old, jnp.max(s, axis=1, keepdims=True))
            top_s[t] = new
            shrink = jnp.exp2((old - new) * c_ref[0])
            p = jnp.exp2((s - new[:, :1]) * c_ref[0]).astype(BF16)
            term = jnp.dot(p, values, preferred_element_type=F32)
            acc_s[t] = acc_s[t] * shrink + term

        s1 = score(queries[1], kv)
        update(0, s_s[...])
        s_s[...] = score(queries[0], pairs(low + jnp.minimum(n + 1, count - 1)))
        update(1, s1)
        return carry

    lax.fori_loop(0, count, step, 0)
    scaled = []
    for t in range(2):
        acc = acc_s[t]
        attended = jnp.where(first, 0.0, acc / acc[:, :1])
        level = jnp.sum(attended * attended, axis=1, keepdims=True) / hs
        scaled.append(attended * lax.rsqrt(level + 1e-05))
    out = jnp.where(first, pltpu.roll(scaled[0], hs, 1), scaled[1])
    o_ref[0] = (out * g_ref[...]).astype(BF16)


def attention(span, c, gain, got, others, tile, hs):
    views, depth, lanes = got.shape
    part = depth - tile
    rows = part * (len(others) + 1)
    whole = lambda i, s: (0, 0, 0)
    work = 2 * tile * views * rows * (views // 2)
    return pl.pallas_call(
        functools.partial(attention_kernel, hs),
        out_shape=jax.ShapeDtypeStruct((views, tile, lanes), BF16),
        grid_spec=pltpu.PrefetchScalarGridSpec(
            num_scalar_prefetch=1,
            grid=(views,),
            in_specs=[
                pl.BlockSpec(memory_space=pltpu.SMEM),
                pl.BlockSpec((1, lanes), lambda i, s: (0, 0)),
                pl.BlockSpec((views, depth, lanes), whole),
            ]
            + [pl.BlockSpec((views, part, lanes), whole) for _ in others],
            out_specs=pl.BlockSpec((1, tile, lanes), lambda i, s: (i, 0, 0)),
            scratch_shapes=[
                pltpu.VMEM((tile, rows), F32),
                pltpu.VMEM((2, tile, lanes), F32),
                pltpu.VMEM((2, tile, lanes), F32),
            ],
        ),
        compiler_params=pltpu.CompilerParams(vmem_limit_bytes=48 << 20),
        cost_estimate=pl.CostEstimate(
            flops=4 * work * lanes, bytes_accessed=8 * views * rows * lanes, transcendentals=work
        ),
    )(span, c, gain, got, *others)


def body(tp, tokens, view_counts, ln_gain, w_qkv, head_temp, o_gain, w_o):
    rows, part = tokens.shape
    me = lax.axis_index("tp")
    swap = [(0, 1), (1, 0)]
    if tp == 2:
        other = lax.ppermute(tokens, "tp", swap)
        whole = jnp.where(
            me == 0,
            jnp.concatenate([tokens, other], axis=1),
            jnp.concatenate([other, tokens], axis=1),
        )
    else:
        whole = lax.all_gather(tokens, "tp", axis=1, tiled=True)
    xfull = whole.astype(F32)
    center = xfull - jnp.mean(xfull, axis=-1, keepdims=True)
    spread = jnp.mean(center * center, axis=-1, keepdims=True)
    normed = (center * lax.rsqrt(spread + 1e-05) * ln_gain).astype(BF16)

    heads_here = head_temp.shape[0]
    width = w_qkv.shape[2]
    hs = width // heads_here
    views = lax.axis_size("ctx")
    split = views // heads_here
    cut = rows // split
    tile = cut // 2
    own_view = lax.axis_index("ctx")
    own_head = own_view // split

    ends = jnp.cumsum(view_counts)
    scene = jnp.sum(
        (ends[None, :] <= jnp.arange(views, dtype=jnp.int32)[:, None]).astype(jnp.int32), axis=1
    )
    counts = view_counts[scene]
    span = jnp.stack([ends[scene] - counts, counts]).astype(jnp.int32)
    c = lax.dynamic_slice_in_dim(head_temp, own_head, 1) * (LOG2E / math.sqrt(hs))
    gain = lax.dynamic_slice_in_dim(o_gain, own_head * hs, hs)
    gain = jnp.concatenate([gain, gain]).reshape(1, 2 * hs)

    depth = w_qkv.shape[1]
    w_kv = jnp.transpose(w_qkv[1:].reshape(2, depth, heads_here, hs), (1, 2, 0, 3))
    kv = jnp.dot(
        normed, w_kv.reshape(depth, 2 * width), preferred_element_type=F32
    ).astype(BF16)
    kv = jnp.transpose(kv.reshape(split, cut, heads_here, 2 * hs), (2, 0, 1, 3))
    query = jnp.dot(normed, w_qkv[0], preferred_element_type=F32).astype(BF16)
    query = jnp.transpose(query.reshape(split, 2, tile, heads_here, hs), (3, 0, 2, 1, 4))
    send = jnp.concatenate(
        [kv.reshape(views, cut, 2 * hs), query.reshape(views, tile, 2 * hs)], axis=1
    )
    got = lax.all_to_all(send, "ctx", split_axis=0, concat_axis=0, tiled=True)
    others = []
    for shift in range(1, split):
        perm = [(v, v // split * split + (v + shift) % split) for v in range(views)]
        others.append(lax.ppermute(got[:, :cut], "ctx", perm))
    if tp == 2:
        out_here = lax.dynamic_slice_in_dim(w_o, me * part, part, axis=1)
        out_there = lax.dynamic_slice_in_dim(w_o, (1 - me) * part, part, axis=1)
        out_there, _ = lax.optimization_barrier((out_there, got))
        out_there = lax.ppermute(out_there, "tp", swap)
    heads = attention(span, c, gain, got, others, tile, hs)
    back = lax.all_to_all(heads, "ctx", split_axis=0, concat_axis=0, tiled=True)
    back = jnp.transpose(back.reshape(heads_here, split, tile, 2, hs), (1, 3, 2, 0, 4))
    back = back.reshape(rows, width)
    total = tokens.astype(F32)
    if tp == 2:
        received = lax.ppermute(back, "tp", swap)
        total = total + jnp.dot(back, out_here, preferred_element_type=F32)
        total = total + jnp.dot(received, out_there, preferred_element_type=F32)
    else:
        terms = jnp.dot(back, w_o, preferred_element_type=F32)
        total = total + lax.psum_scatter(
            terms.astype(BF16), "tp", scatter_dimension=1, tiled=True
        ).astype(F32)
    return total.astype(BF16)


def solution(mesh):
    in_specs = (P("ctx", "tp"), P(), P(), P(None, None, "tp"), P("tp"), P("tp"), P("tp", None))
    out_specs = P("ctx", "tp")
    return jax.shard_map(
        functools.partial(body, mesh.shape["tp"]),
        mesh=mesh,
        in_specs=in_specs,
        out_specs=out_specs,
        check_vma=False,
    )
```

```python
import functools
import math

import jax
import jax.numpy as jnp
from jax import lax
from jax.experimental import pallas as pl
from jax.experimental.pallas import tpu as pltpu
from jax.sharding import PartitionSpec as P

BF16 = jnp.bfloat16
F32 = jnp.float32
LOG2E = 1.4426950408889634


def attention_kernel(hs, span, c_ref, g_ref, got_ref, *rest):
    *others, o_ref, s_s, top_s, acc_s = rest
    i = pl.program_id(0)
    tile, lanes = o_ref.shape[1:]
    part = got_ref.shape[1] - tile
    first = lax.broadcasted_iota(jnp.int32, (tile, lanes), 1) < hs
    packed = got_ref[i, part:, :].astype(F32)
    queries = [
        jnp.where(first, x, 0.0).astype(BF16) for x in (packed, pltpu.roll(packed, hs, 1))
    ]
    low, count = span[0, i], span[1, i]

    def pairs(j):
        return jnp.concatenate([got_ref[j, :part, :]] + [ref[j] for ref in others], axis=0)

    def score(query, kv):
        return lax.dot_general(
            query, kv, (((1,), (1,)), ((), ())), preferred_element_type=F32
        )

    top_s[...] = jnp.full_like(top_s, -1e30)
    acc_s[...] = jnp.zeros_like(acc_s)
    s_s[...] = score(queries[0], pairs(low))

    def step(n, carry):
        kv = pairs(low + n)
        key_lanes = lax.broadcasted_iota(jnp.int32, kv.shape, 1) < hs
        values = jnp.where(key_lanes, jnp.ones((), BF16), kv)

        def update(t, s):
            old = top_s[t]
            new = jnp.maximum(old, jnp.max(s, axis=1, keepdims=True))
            top_s[t] = new
            shrink = jnp.exp2((old - new) * c_ref[0])
            p = jnp.exp2((s - new[:, :1]) * c_ref[0]).astype(BF16)
            term = jnp.dot(p, values, preferred_element_type=F32)
            acc_s[t] = acc_s[t] * shrink + term

        s1 = score(queries[1], kv)
        update(0, s_s[...])
        s_s[...] = score(queries[0], pairs(low + jnp.minimum(n + 1, count - 1)))
        update(1, s1)
        return carry

    lax.fori_loop(0, count, step, 0)
    scaled = []
    for t in range(2):
        acc = acc_s[t]
        attended = jnp.where(first, 0.0, acc / acc[:, :1])
        level = jnp.sum(attended * attended, axis=1, keepdims=True) / hs
        scaled.append(attended * lax.rsqrt(level + 1e-05))
    out = jnp.where(first, pltpu.roll(scaled[0], hs, 1), scaled[1])
    o_ref[0] = (out * g_ref[...]).astype(BF16)


def attention(span, c, gain, got, others, tile, hs):
    views, depth, lanes = got.shape
    part = depth - tile
    rows = part * (len(others) + 1)
    whole = lambda i, s: (0, 0, 0)
    work = 2 * tile * views * rows * (views // 2)
    return pl.pallas_call(
        functools.partial(attention_kernel, hs),
        out_shape=jax.ShapeDtypeStruct((views, tile, lanes), BF16),
        grid_spec=pltpu.PrefetchScalarGridSpec(
            num_scalar_prefetch=1,
            grid=(views,),
            in_specs=[
                pl.BlockSpec(memory_space=pltpu.SMEM),
                pl.BlockSpec((1, lanes), lambda i, s: (0, 0)),
                pl.BlockSpec((views, depth, lanes), whole),
            ]
            + [pl.BlockSpec((views, part, lanes), whole) for _ in others],
            out_specs=pl.BlockSpec((1, tile, lanes), lambda i, s: (i, 0, 0)),
            scratch_shapes=[
                pltpu.VMEM((tile, rows), F32),
                pltpu.VMEM((2, tile, lanes), F32),
                pltpu.VMEM((2, tile, lanes), F32),
            ],
        ),
        compiler_params=pltpu.CompilerParams(vmem_limit_bytes=48 << 20),
        cost_estimate=pl.CostEstimate(
            flops=4 * work * lanes, bytes_accessed=8 * views * rows * lanes, transcendentals=work
        ),
    )(span, c, gain, got, *others)


def body(tp, tokens, view_counts, ln_gain, w_qkv, head_temp, o_gain, w_o):
    rows, part = tokens.shape
    me = lax.axis_index("tp")
    swap = [(0, 1), (1, 0)]
    if tp == 2:
        other = lax.ppermute(tokens, "tp", swap)
        whole = jnp.where(
            me == 0,
            jnp.concatenate([tokens, other], axis=1),
            jnp.concatenate([other, tokens], axis=1),
        )
    else:
        whole = lax.all_gather(tokens, "tp", axis=1, tiled=True)
    if tp == 2:
        out_here = lax.dynamic_slice_in_dim(w_o, me * part, part, axis=1)
        out_there = lax.dynamic_slice_in_dim(w_o, (1 - me) * part, part, axis=1)
        out_there, whole = lax.optimization_barrier((out_there, whole))
        out_there = lax.ppermute(out_there, "tp", swap)
    xfull = whole.astype(F32)
    center = xfull - jnp.mean(xfull, axis=-1, keepdims=True)
    spread = jnp.mean(center * center, axis=-1, keepdims=True)
    normed = (center * lax.rsqrt(spread + 1e-05) * ln_gain).astype(BF16)

    heads_here = head_temp.shape[0]
    width = w_qkv.shape[2]
    hs = width // heads_here
    views = lax.axis_size("ctx")
    split = views // heads_here
    cut = rows // split
    tile = cut // 2
    own_view = lax.axis_index("ctx")
    own_head = own_view // split

    ends = jnp.cumsum(view_counts)
    scene = jnp.sum(
        (ends[None, :] <= jnp.arange(views, dtype=jnp.int32)[:, None]).astype(jnp.int32), axis=1
    )
    counts = view_counts[scene]
    span = jnp.stack([ends[scene] - counts, counts]).astype(jnp.int32)
    c = lax.dynamic_slice_in_dim(head_temp, own_head, 1) * (LOG2E / math.sqrt(hs))
    gain = lax.dynamic_slice_in_dim(o_gain, own_head * hs, hs)
    gain = jnp.concatenate([gain, gain]).reshape(1, 2 * hs)

    depth = w_qkv.shape[1]
    w_kv = jnp.transpose(w_qkv[1:].reshape(2, depth, heads_here, hs), (1, 2, 0, 3))
    kv = jnp.dot(
        normed, w_kv.reshape(depth, 2 * width), preferred_element_type=F32
    ).astype(BF16)
    kv = jnp.transpose(kv.reshape(split, cut, heads_here, 2 * hs), (2, 0, 1, 3))
    query = jnp.dot(normed, w_qkv[0], preferred_element_type=F32).astype(BF16)
    query = jnp.transpose(query.reshape(split, 2, tile, heads_here, hs), (3, 0, 2, 1, 4))
    send = jnp.concatenate(
        [kv.reshape(views, cut, 2 * hs), query.reshape(views, tile, 2 * hs)], axis=1
    )
    got = lax.all_to_all(send, "ctx", split_axis=0, concat_axis=0, tiled=True)
    if tp == 2:
        got, out_there = lax.optimization_barrier((got, out_there))
    others = []
    for shift in range(1, split):
        perm = [(v, v // split * split + (v + shift) % split) for v in range(views)]
        others.append(lax.ppermute(got[:, :cut], "ctx", perm))
    heads = attention(span, c, gain, got, others, tile, hs)
    back = lax.all_to_all(heads, "ctx", split_axis=0, concat_axis=0, tiled=True)
    back = jnp.transpose(back.reshape(heads_here, split, tile, 2, hs), (1, 3, 2, 0, 4))
    back = back.reshape(rows, width)
    total = tokens.astype(F32)
    if tp == 2:
        received = lax.ppermute(back, "tp", swap)
        total = total + jnp.dot(back, out_here, preferred_element_type=F32)
        total = total + jnp.dot(received, out_there, preferred_element_type=F32)
    else:
        terms = jnp.dot(back, w_o, preferred_element_type=F32)
        total = total + lax.psum_scatter(
            terms.astype(BF16), "tp", scatter_dimension=1, tiled=True
        ).astype(F32)
    return total.astype(BF16)


def solution(mesh):
    in_specs = (P("ctx", "tp"), P(), P(), P(None, None, "tp"), P("tp"), P("tp"), P("tp", None))
    out_specs = P("ctx", "tp")
    return jax.shard_map(
        functools.partial(body, mesh.shape["tp"]),
        mesh=mesh,
        in_specs=in_specs,
        out_specs=out_specs,
        check_vma=False,
    )
```
